128 devices in a mesh: ctx: 16 (over x, y), head: 8 (over z, core).
Axes of the slice: x: 4, y: 4, z: 4, core: 2. Of those that a mesh axis runs over, the one named last changes fastest.
Arguments:
- queries: bfloat16 [16384, 4096], P(('ctx', 'head')), may hold values from -12 to 12
- keys: bfloat16 [16384, 4096], P(('ctx', 'head')), may hold values from -6 to 6
- values: bfloat16 [16384, 4096], P(('ctx', 'head')), may hold values from -6 to 6
- grad_out: bfloat16 [16384, 4096], P(('ctx', 'head')), may hold values from -6 to 6
- local_blocks: int32 [128, 4], P('ctx'), may hold values from 0 to 7, as said below
- summary_blocks: int32 [16, 1], P('ctx'), may hold values from 0 to 7, as said below
Outputs:
- attended: bfloat16 [16384, 4096], P(('ctx', 'head'))
- grad_queries: bfloat16 [16384, 4096], P(('ctx', 'head'))
- grad_keys: bfloat16 [16384, 4096], P(('ctx', 'head'))
- grad_values: bfloat16 [16384, 4096], P(('ctx', 'head'))
The draws below stay inside these ranges and needn't reach their ends.
Inputs may be any that keep to these rules, and one draw needn't show every extreme that they name: `local_blocks`: each row names 4 different blocks, numbered within the query block's own span; its first entry is the query block itself. `summary_blocks`: each row names the one block of that span that serves as its summary, numbered within that span.
All inputs are finite; a program needn't handle non-finite values.
Results may differ from the reference program's by a relative error of at most 0.015.
Values may be sent and summed in bfloat16 or wider, within the bound.
No kernel may reach another device: no remote copies, remote signals or barrier semaphores. Data moves between devices by JAX's collectives and lax.ppermute only.
A program may use at most 128 MiB of HBM per device.

```python
from functools import partial
import jax
import jax.numpy as jnp
from jax import lax

H = 32
DH = 128
BLK = 128
NLOC = 4
NSUM = 1
D = 4096
SPAN = 1024
SEQ = 16384
N_CTX = 16


def draw_queries(key, part):
    key = jax.random.fold_in(key, 11)
    entries = jnp.clip(2.0 * jax.random.normal(key, (SEQ, H * DH), jnp.float32), -12.0, 12.0)
    return entries.astype(jnp.bfloat16)


def draw_keys(key, part):
    key = jax.random.fold_in(key, 13)
    entries = jnp.clip(jax.random.normal(key, (SEQ, H * DH), jnp.float32), -6.0, 6.0)
    return entries.astype(jnp.bfloat16)


def draw_local_blocks(key, part):
    key = jax.random.fold_in(key, 5)
    nblocks = SPAN // BLK
    row_count = N_CTX * nblocks
    row_keys = jax.random.split(key, row_count)
    offsets = jax.vmap(lambda sub_key: jax.random.permutation(sub_key, nblocks - 1))(row_keys)[:, :NLOC - 1] + 1
    offsets = jnp.concatenate([jnp.zeros((row_count, 1), jnp.int32), offsets.astype(jnp.int32)], 1)
    block_ids = (jnp.arange(row_count, dtype=jnp.int32) % nblocks)[:, None]
    return ((block_ids + offsets) % nblocks).astype(jnp.int32)


def draw_summary_blocks(key, part):
    key = jax.random.fold_in(key, 7)
    nblocks = SPAN // BLK
    row_key, pick_key, other_key = jax.random.split(key, 3)
    row_keys = jax.random.split(row_key, N_CTX)
    chosen = jax.vmap(lambda sub_key: jax.random.permutation(sub_key, nblocks))(row_keys)[:, :NSUM].astype(jnp.int32)
    top_span = jax.random.randint(pick_key, (), 0, N_CTX)
    low_span = (top_span + 1 + jax.random.randint(other_key, (), 0, N_CTX - 1)) % N_CTX
    chosen = chosen.at[top_span].set(jnp.arange(NSUM, dtype=jnp.int32) + nblocks - NSUM)
    chosen = chosen.at[low_span].set(jnp.arange(NSUM, dtype=jnp.int32))
    return chosen.astype(jnp.int32)


def levels(key, dims, cuts, least, high):
    factor_of, own = 1.0, jax.random.fold_in(key, 6)
    for dim, blocks in cuts:
        heights = jnp.exp(jax.random.uniform(jax.random.fold_in(own, dim), (blocks,), jnp.float32, least / len(cuts), high / len(cuts)))
        factor_of = factor_of * jnp.repeat(heights, dims[dim] // blocks).reshape([-1 if axis == dim else 1 for axis in range(len(dims))])
    return factor_of


def centred(own_key, dims, width, most, pieces=(), kind=jnp.bfloat16):
    level = levels(own_key, dims, pieces, -0.22, 0.18) if pieces else 1.0
    drawn = jax.random.normal(own_key, dims, jnp.float32) * width * level
    return jnp.minimum(jnp.maximum(drawn, -most), most).astype(kind)


def setup_inputs(seed: int = 0) -> dict:
    splits = jax.random.split(jax.random.key(seed), 7)
    queries = draw_queries(jax.random.fold_in(splits[6], 71), 0)
    keys = draw_keys(jax.random.fold_in(splits[6], 71), 0)
    values = centred(splits[2], (SEQ, D), 1.0, 6.0, ((0, 128),))
    grad_out = centred(splits[3], (SEQ, D), 1.0, 6.0, ((0, 128),))
    local_blocks = draw_local_blocks(jax.random.fold_in(splits[6], 71), 0)
    summary_blocks = draw_summary_blocks(jax.random.fold_in(splits[6], 71), 0)
    return dict(queries=queries, keys=keys, values=values, grad_out=grad_out, local_blocks=local_blocks, summary_blocks=summary_blocks)


NEGATIVE_PADDING = -1.0e30


def multiplied_result(form, left, right):
    return jnp.einsum(form, left.astype(jnp.float32), right.astype(jnp.float32))


def rounded(matrix):
    return lax.optimization_barrier(matrix.astype(jnp.bfloat16))


def split_heads(matrix, head_count):
    return matrix.reshape(matrix.shape[0], head_count, -1).transpose(1, 0, 2)


def head_pass(inputs, valid_mask, logit_scale):
    head_queries, nearby_keys, nearby_values, distant_keys, distant_values, upstream_gradient = inputs
    nearby_logits = multiplied_result("cgu,cfu->cgf", head_queries, nearby_keys) * logit_scale
    distant_logits = jnp.where(valid_mask, multiplied_result("xra,ga->xrg", head_queries, distant_keys) * logit_scale, NEGATIVE_PADDING)
    row_top = jnp.maximum(nearby_logits.max(-1), distant_logits.max(-1))
    row_total = jnp.exp(nearby_logits - row_top[..., None]).sum(-1) + jnp.exp(distant_logits - row_top[..., None]).sum(-1)
    log_total = row_top + jnp.log(row_total)
    near_p = jnp.exp(nearby_logits - log_total[..., None])
    far_p = jnp.exp(distant_logits - log_total[..., None])
    nearby_probs = rounded(near_p)
    distant_probs = rounded(far_p)
    attended = (multiplied_result("ufm,umo->ufo", nearby_probs, nearby_values) + multiplied_result("egz,zy->egy", distant_probs, distant_values)).astype(jnp.bfloat16)
    delta = jnp.sum(upstream_gradient.astype(jnp.float32) * attended.astype(jnp.float32), -1)
    nearby_prob_gradient = multiplied_result("cgu,cfu->cgf", upstream_gradient, nearby_values)
    distant_prob_gradient = multiplied_result("xra,ga->xrg", upstream_gradient, distant_values)
    nearby_score_gradient = rounded(near_p * (nearby_prob_gradient - delta[..., None]) * logit_scale)
    distant_score_gradient = rounded(far_p * (distant_prob_gradient - delta[..., None]) * logit_scale)
    query_gradient = (multiplied_result("ufm,umo->ufo", nearby_score_gradient, nearby_keys) + multiplied_result("egz,zy->egy", distant_score_gradient, distant_keys)).astype(jnp.bfloat16)
    nearby_key_gradient = multiplied_result("enp,ens->eps", nearby_score_gradient, head_queries)
    nearby_value_gradient = multiplied_result("enp,ens->eps", nearby_probs, upstream_gradient)
    distant_key_gradient = multiplied_result("fce,fcx->ex", distant_score_gradient, head_queries)
    distant_value_gradient = multiplied_result("fce,fcx->ex", distant_probs, upstream_gradient)
    return attended, query_gradient, nearby_key_gradient, nearby_value_gradient, distant_key_gradient, distant_value_gradient


def reference(queries, keys, values, grad_out, local_blocks, summary_blocks):
    logit_scale = DH ** -0.5
    nblocks = SPAN // BLK
    features = H * DH
    summary_len = NSUM * BLK
    near_len = NLOC * BLK
    q_spans = queries.reshape(N_CTX, SPAN, features)
    k_spans = keys.reshape(N_CTX, SPAN, features)
    v_spans = values.reshape(N_CTX, SPAN, features)
    g_spans = grad_out.reshape(N_CTX, SPAN, features)
    span_ids = jnp.arange(N_CTX, dtype=jnp.int32)
    sum_k = keys.reshape(N_CTX, nblocks, BLK, features)[span_ids[:, None], summary_blocks].reshape(-1, features)
    sum_v = values.reshape(N_CTX, nblocks, BLK, features)[span_ids[:, None], summary_blocks].reshape(-1, features)
    distant_keys = split_heads(sum_k, H)
    distant_values = split_heads(sum_v, H)
    local_rows = local_blocks.reshape(N_CTX, nblocks, NLOC)

    def per_head(matrix, block_len):
        return split_heads(matrix, H).reshape(H, -1, block_len, DH)

    def span_step(running, span_index):
        far_dk, far_dv = running
        near_picks = local_rows[span_index]
        head_queries = per_head(q_spans[span_index], BLK)
        upstream_gradient = per_head(g_spans[span_index], BLK)
        nearby_keys = per_head(k_spans[span_index].reshape(nblocks, BLK, features)[near_picks].reshape(-1, features), near_len)
        nearby_values = per_head(v_spans[span_index].reshape(nblocks, BLK, features)[near_picks].reshape(-1, features), near_len)
        valid_mask = (jnp.arange(N_CTX * summary_len, dtype=jnp.int32) // summary_len) < span_index
        results = lax.map(partial(head_pass, valid_mask=valid_mask, logit_scale=logit_scale), (head_queries, nearby_keys, nearby_values, distant_keys, distant_values, upstream_gradient))
        attended, query_gradient, nearby_key_gradient, nearby_value_gradient, distant_key_gradient, distant_value_gradient = results
        placing = (near_picks.reshape(-1)[None, :] == jnp.arange(nblocks, dtype=jnp.int32)[:, None]).astype(jnp.float32)
        dk_local = multiplied_result("tj,hjx->htx", placing, nearby_key_gradient.reshape(H, -1, BLK * DH))
        dv_local = multiplied_result("tj,hjx->htx", placing, nearby_value_gradient.reshape(H, -1, BLK * DH))
        far_dk = far_dk + rounded(distant_key_gradient).astype(jnp.float32)
        far_dv = far_dv + rounded(distant_value_gradient).astype(jnp.float32)
        return (far_dk, far_dv), (attended, query_gradient, dk_local, dv_local)

    start = (jnp.zeros((H, N_CTX * summary_len, DH), jnp.float32), jnp.zeros((H, N_CTX * summary_len, DH), jnp.float32))
    (far_dk, far_dv), stacked = lax.scan(span_step, start, span_ids)
    attended, query_gradient, dk_local, dv_local = stacked

    def to_rows(block):
        return block.reshape(N_CTX, H, nblocks, BLK, DH).transpose(0, 2, 3, 1, 4)

    def finish(local_part, far_part):
        far_rows = far_part.transpose(1, 0, 2).reshape(N_CTX, NSUM, BLK, H, DH)
        whole = to_rows(local_part).at[span_ids[:, None], summary_blocks].add(far_rows)
        return whole.astype(jnp.bfloat16).reshape(SEQ, features)

    return (to_rows(attended).reshape(SEQ, features), to_rows(query_gradient).reshape(SEQ, features),
            finish(dk_local, far_dk), finish(dv_local, far_dv))
```

```python
import jax
import jax.numpy as jnp
from jax import lax
from jax.experimental import pallas as pl
from jax.experimental.pallas import tpu as pltpu
from jax.sharding import PartitionSpec as P

BLK = 128
NB = 8
SPAN = 1024
SCALE = 128 ** -0.5
LOG2E = 1.4426950408889634
NEG = -1e30
QT = 256
bf16 = jnp.bfloat16
f32 = jnp.float32


def dot_nt(a, b):
    return lax.dot_general(a, b, (((1,), (1,)), ((), ())), preferred_element_type=f32)


def dot_nn(a, b):
    return lax.dot_general(a, b, (((1,), (0,)), ((), ())), preferred_element_type=f32)


def fold_max(s):
    return s.reshape(s.shape[0] // 8, 8, s.shape[1]).max(0)


def fold_sum(s):
    return s.reshape(s.shape[0] // 8, 8, s.shape[1]).sum(0)


def attention_kernel(
    pos, local, kv, qg, k0, k1, k2, k3, v0, v1, v2, v3,
    ao, dl, dsum, fk, fv,
    kf, vf, kt, vt, kl, vl, klt, vlt, s_ref, p_ref, d_ref, mx, sm, ot, dqt, dk_acc, dv_acc, gs, qs,
):
    x, y, sb = pos[0], pos[1], pos[2]
    ks, vs = (k0, k1, k2, k3), (v0, v1, v2, v3)
    for sx in range(4):
        for sy in range(4):
            kf[sx, sy * BLK:(sy + 1) * BLK, :] = ks[sx][sy]
            vf[sx, sy * BLK:(sy + 1) * BLK, :] = vs[sy][sx]
    mx[...] = jnp.full_like(mx, NEG)
    sm[...] = jnp.zeros_like(sm)
    ot[...] = jnp.zeros_like(ot)
    dqt[...] = jnp.zeros_like(dqt)
    dk_acc[...] = jnp.zeros_like(dk_acc)
    dv_acc[...] = jnp.zeros_like(dv_acc)

    def queries(t, n=2):
        return qg[t * n:(t + 1) * n, 0].reshape(n * BLK, BLK)

    def cots(t, n=2):
        return qg[t * n:(t + 1) * n, 1].reshape(n * BLK, BLK)

    def score_far(sx, first):
        kt[sx] = kf[sx].T
        vt[sx] = vf[sx].T
        for t in range(4):
            cols = slice(t * QT, (t + 1) * QT)
            s = dot_nt(kf[sx], queries(t))
            s_ref[sx, :, cols] = s
            if first:
                top = jnp.full((8, QT), NEG, f32)
                for sy in range(1, 4):
                    top = jnp.maximum(top, jnp.where(sy <= y, fold_max(s[sy * BLK:(sy + 1) * BLK]), NEG))
            else:
                top = fold_max(s)
            mx[:, cols] = jnp.maximum(mx[:, cols], top)

    score_far(0, True)
    pl.loop(1, x + 1)(lambda sx: score_far(sx, False))

    @pl.loop(0, NB)
    def _(b):
        for i in range(4):
            idx = local[b * 4 + i]
            kl[b, i * BLK:(i + 1) * BLK, :] = kv[idx, 0]
            vl[b, i * BLK:(i + 1) * BLK, :] = kv[idx, 1]
        klt[b] = kl[b].T
        vlt[b] = vl[b].T
        cols = pl.ds(pl.multiple_of(b * BLK, BLK), BLK)
        s = dot_nt(kl[b], qg[b, 0])
        s_ref[4, :, cols] = s
        mx[:, cols] = jnp.maximum(mx[:, cols], fold_max(s))

    mc = mx[...].max(0, keepdims=True) * (SCALE * LOG2E)

    def prob_far(sx, first):
        for t in range(4):
            cols = slice(t * QT, (t + 1) * QT)
            total = sm[:, cols]
            for sy in range(4):
                rows = slice(sy * BLK, (sy + 1) * BLK)
                shift = mc[:, cols]
                if first:
                    shift = jnp.where((sy >= 1) & (sy <= y), shift, -NEG)
                p = jnp.exp2(s_ref[sx, rows, cols] * (SCALE * LOG2E) - shift)
                total = total + fold_sum(p)
                p_ref[sx, rows, cols] = p.astype(bf16)
            sm[:, cols] = total
            ot[:, cols] += dot_nn(vt[sx], p_ref[sx, :, cols])

    prob_far(0, True)
    pl.loop(1, x + 1)(lambda sx: prob_far(sx, False))
    for b in range(NB):
        cols = slice(b * BLK, (b + 1) * BLK)
        p = jnp.exp2(s_ref[4, :, cols] * (SCALE * LOG2E) - mc[:, cols])
        sm[:, cols] += fold_sum(p)
        p_ref[4, :, cols] = p.astype(bf16)
        ot[:, cols] += dot_nn(vlt[b], p_ref[4, :, cols])

    inv = 1.0 / sm[...].sum(0, keepdims=True)
    deltas = []
    for b in range(NB):
        cols = slice(b * BLK, (b + 1) * BLK)
        o = (ot[:, cols] * inv[:, cols]).T.astype(bf16)
        ao[b, 0] = o
        g = qg[b, 1].astype(f32)
        column = jnp.broadcast_to(inv[:, cols], (BLK, BLK)).T
        gs[cols, :] = (g * column).astype(bf16)
        qs[cols, :] = (qg[b, 0].astype(f32) * (column * SCALE)).astype(bf16)
        deltas.append((g * o.astype(f32)).T.sum(0, keepdims=True))
    delta = jnp.concatenate(deltas, 1)

    def grad_far(sx):
        for t in range(4):
            cols = slice(t * QT, (t + 1) * QT)
            dp = dot_nt(vf[sx], cots(t))
            for sy in range(4):
                rows = slice(sy * BLK, (sy + 1) * BLK)
                d_ref[sx, rows, cols] = p_ref[sx, rows, cols] * (dp[rows] - delta[:, cols]).astype(bf16)
            dqt[:, cols] += dot_nn(kt[sx], d_ref[sx, :, cols])
        fv[:, sx] = dot_nn(p_ref[sx], gs[...]).reshape(4, BLK, BLK).astype(bf16)
        fk[sx] = dot_nn(d_ref[sx], qs[...]).reshape(4, BLK, BLK).astype(bf16)

    pl.loop(0, x + 1)(grad_far)
    for b in range(NB):
        cols = slice(b * BLK, (b + 1) * BLK)
        dp = dot_nt(vl[b], qg[b, 1])
        d_ref[4, :, cols] = p_ref[4, :, cols] * (dp - delta[:, cols]).astype(bf16)
        dqt[:, cols] += dot_nn(klt[b], d_ref[4, :, cols])
        dv = dot_nn(p_ref[4, :, cols], gs[cols, :])
        dk = dot_nn(d_ref[4, :, cols], qs[cols, :])
        for i in range(4):
            idx = local[b * 4 + i]
            dk_acc[idx] += dk[i * BLK:(i + 1) * BLK]
            dv_acc[idx] += dv[i * BLK:(i + 1) * BLK]
        ao[b, 1] = (dqt[:, cols] * (inv[:, cols] * SCALE)).T.astype(bf16)
    dl[:, 0] = dk_acc[...].astype(bf16)
    dl[:, 1] = dv_acc[...].astype(bf16)
    dsum[0] = dk_acc[sb]
    dsum[1] = dv_acc[sb]


def attention(pos, local, kv, qg, ks, vs):
    width = kv.shape[-1]
    heads = width // BLK
    pair = pl.BlockSpec((NB, 2, BLK, BLK), lambda h: (0, 0, 0, h))
    far = pl.BlockSpec((4, BLK, BLK), lambda h: (0, 0, h))
    smem = pl.BlockSpec(memory_space=pltpu.SMEM)
    return pl.pallas_call(
        attention_kernel,
        grid=(heads,),
        in_specs=[smem, smem, pair, pair] + [far] * 8,
        out_specs=[
            pair, pair,
            pl.BlockSpec((2, BLK, BLK), lambda h: (0, 0, h)),
            pl.BlockSpec((4, 4, BLK, BLK), lambda h: (0, 0, 0, h)),
            pl.BlockSpec((4, 4, BLK, BLK), lambda h: (0, 0, 0, h)),
        ],
        out_shape=[
            jax.ShapeDtypeStruct((NB, 2, BLK, width), bf16),
            jax.ShapeDtypeStruct((NB, 2, BLK, width), bf16),
            jax.ShapeDtypeStruct((2, BLK, width), f32),
            jax.ShapeDtypeStruct((4, 4, BLK, width), bf16),
            jax.ShapeDtypeStruct((4, 4, BLK, width), bf16),
        ],
        scratch_shapes=[
            pltpu.VMEM((4, 512, BLK), bf16), pltpu.VMEM((4, 512, BLK), bf16),
            pltpu.VMEM((4, BLK, 512), bf16), pltpu.VMEM((4, BLK, 512), bf16),
            pltpu.VMEM((NB, 512, BLK), bf16), pltpu.VMEM((NB, 512, BLK), bf16),
            pltpu.VMEM((NB, BLK, 512), bf16), pltpu.VMEM((NB, BLK, 512), bf16),
            pltpu.VMEM((5, 512, SPAN), f32), pltpu.VMEM((5, 512, SPAN), bf16), pltpu.VMEM((5, 512, SPAN), bf16),
            pltpu.VMEM((8, SPAN), f32), pltpu.VMEM((8, SPAN), f32),
            pltpu.VMEM((BLK, SPAN), f32), pltpu.VMEM((BLK, SPAN), f32),
            pltpu.VMEM((NB, BLK, BLK), f32), pltpu.VMEM((NB, BLK, BLK), f32),
            pltpu.VMEM((SPAN, BLK), bf16), pltpu.VMEM((SPAN, BLK), bf16),
        ],
        compiler_params=pltpu.CompilerParams(vmem_limit_bytes=56 << 20),
        cost_estimate=pl.CostEstimate(flops=heads * 12 * SPAN * 2432 * BLK, bytes_accessed=heads * (4 << 20), transcendentals=heads * SPAN * 2432),
    )(pos, local, kv, qg, *ks, *vs)


SIDE = 4


def along_x(array, step, rows=range(SIDE), wrap=False):
    pairs = []
    for x in rows:
        to = x + step
        if wrap:
            to %= SIDE
        if 0 <= to < SIDE:
            pairs += [(x * SIDE + y, to * SIDE + y) for y in range(SIDE)]
    return lax.ppermute(array, "ctx", pairs)


def along_y(array, step):
    return lax.ppermute(
        array, "ctx", [(x * SIDE + y, x * SIDE + (y + step) % SIDE) for x in range(SIDE) for y in range(SIDE)]
    )


def gather_keys(own):
    row = jnp.stack([own] + [along_y(own, s) for s in (1, 2, 3)])
    near = along_x(row, 1)
    last = along_x(row, 3)
    return (row, near, along_x(near, 1, (1, 2)), last)


def gather_values(own):
    column = jnp.stack([own] + [along_x(own, s) for s in (1, 2, 3)])
    near = along_y(column, 1)
    last = along_y(column, -1)
    return (column, near, along_y(near, 1), last)


def plus(*terms):
    total = terms[0].astype(f32)
    for term in terms[1:]:
        total = total + term.astype(f32)
    return total


def scatter_keys(parts):
    passed = along_x(parts[2], -1, (3, 2))
    last = along_x(parts[3], -3)
    near = along_x(plus(parts[1], passed).astype(bf16), -1)
    row = plus(parts[0], near, last).astype(bf16)
    return plus(row[0], *[along_y(row[s], -s) for s in (1, 2, 3)])


def scatter_values(parts):
    passed = along_y(parts[2], -1)
    last = along_y(parts[3], 1)
    near = along_y(plus(parts[1], passed).astype(bf16), -1)
    column = plus(parts[0], near, last).astype(bf16)
    return plus(column[0], *[along_x(column[s], -s) for s in (1, 2, 3)])


def exchange(array):
    return lax.all_to_all(array, "head", split_axis=0, concat_axis=0, tiled=True)


def to_groups(a, b):
    def cut(m):
        return m.reshape(BLK, NB, -1).transpose(1, 0, 2)

    return exchange(jnp.stack([cut(a), cut(b)], 1))


def to_tokens(pair):
    got = exchange(pair)
    return tuple(got[:, i].transpose(1, 0, 2).reshape(BLK, -1) for i in range(2))


def device_step(queries, keys, values, grad_out, local_blocks, summary_blocks):
    j = lax.axis_index("ctx")
    sb = summary_blocks[0, 0]
    kv = to_groups(keys, values)
    qg = to_groups(queries, grad_out)
    own = lax.dynamic_index_in_dim(kv, sb, 0, keepdims=False)
    ks = gather_keys(own[0])
    vs = gather_values(own[1])
    pos = jnp.stack([j // SIDE, j % SIDE, sb]).astype(jnp.int32)
    ao, dl, dsum, fk, fv = attention(pos, local_blocks.reshape(-1), kv, qg, ks, vs)
    attended, grad_q = to_tokens(ao)
    own_grad = (dsum + jnp.stack([scatter_keys(fk), scatter_values(fv)])).astype(bf16)
    dl = lax.dynamic_update_slice(dl, own_grad[None], (sb, 0, 0, 0))
    grad_k, grad_v = to_tokens(dl)
    return attended, grad_q, grad_k, grad_v


def solution(mesh):
    tokens = P(("ctx", "head"), None)
    return jax.shard_map(
        device_step,
        mesh=mesh,
        in_specs=(tokens,) * 4 + (P("ctx", None),) * 2,
        out_specs=(tokens,) * 4,
        check_vma=False,
    )
```

```python
import jax
import jax.numpy as jnp
from jax import lax
from jax.experimental import pallas as pl
from jax.experimental.pallas import tpu as pltpu
from jax.sharding import PartitionSpec as P

BLK = 128
NB = 8
SPAN = 1024
SCALE = 128 ** -0.5
LOG2E = 1.4426950408889634
NEG = -1e30
QT = 256
bf16 = jnp.bfloat16
f32 = jnp.float32


def dot_nt(a, b):
    return lax.dot_general(a, b, (((1,), (1,)), ((), ())), preferred_element_type=f32)


def dot_nn(a, b):
    return lax.dot_general(a, b, (((1,), (0,)), ((), ())), preferred_element_type=f32)


def fold_max(s):
    return s.reshape(s.shape[0] // 8, 8, s.shape[1]).max(0)


def fold_sum(s):
    return s.reshape(s.shape[0] // 8, 8, s.shape[1]).sum(0)


def attention_kernel(
    local, summary, kv, qg, k0, k1, k2a, k2b, k3, v0, v1, v2a, v2b, v3,
    ao, dl, dsum, gk0, gk1, gk2a, gk2b, gk3, gv0, gv1, gv2a, gv2b, gv3,
    kf, vf, kt, vt, kl, vl, klt, vlt, s_ref, dp_ref, p_ref, d_ref, mx, sm, ot, dqt, dk_acc, dv_acc, gs, qs, fk, fv,
):
    span = lax.axis_index("ctx")
    x, y, sb = lax.div(span, 4), lax.rem(span, 4), summary[0, 0]
    for a in range(4):
        for c in range(4):
            rows = slice(c * BLK, (c + 1) * BLK)
            kf[a, rows, :] = ((k0, k1, k2a, k3)[a][c] if a != 2 or c < 2 else k2b[c - 2])
            rows = slice(a * BLK, (a + 1) * BLK)
            vf[c, rows, :] = ((v0, v1, v2a, v3)[a][c] if a != 2 or c < 2 else v2b[c - 2])
    fk[...] = jnp.zeros_like(fk)
    fv[...] = jnp.zeros_like(fv)
    mx[...] = jnp.full_like(mx, NEG)
    sm[...] = jnp.zeros_like(sm)
    ot[...] = jnp.zeros_like(ot)
    dqt[...] = jnp.zeros_like(dqt)
    dk_acc[...] = jnp.zeros_like(dk_acc)
    dv_acc[...] = jnp.zeros_like(dv_acc)

    def queries(t, n=2):
        return qg[t * n:(t + 1) * n, 0].reshape(n * BLK, BLK)

    def cots(t, n=2):
        return qg[t * n:(t + 1) * n, 1].reshape(n * BLK, BLK)

    def score_far(sx, first):
        kt[sx] = kf[sx].T
        vt[sx] = vf[sx].T
        for t in range(4):
            cols = slice(t * QT, (t + 1) * QT)
            lo = BLK if first else 0
            s = dot_nt(kf[sx, lo:], queries(t))
            s_ref[sx, lo:, cols] = s
            if first:
                top = jnp.full((8, QT), NEG, f32)
                for sy in range(1, 4):
                    top = jnp.maximum(top, jnp.where(sy <= y, fold_max(s[sy * BLK - lo:(sy + 1) * BLK - lo]), NEG))
            else:
                top = fold_max(s)
            mx[:, cols] = jnp.maximum(mx[:, cols], top)

    score_far(0, True)
    pl.loop(1, x + 1)(lambda sx: score_far(sx, False))

    def local_scores(b):
        for i in range(4):
            idx = local[b, i]
            kl[b, i * BLK:(i + 1) * BLK, :] = kv[idx, 0]
            vl[b, i * BLK:(i + 1) * BLK, :] = kv[idx, 1]
        klt[b] = kl[b].T
        vlt[b] = vl[b].T
        cols = slice(b * BLK, (b + 1) * BLK)
        s = dot_nt(kl[b], qg[b, 0])
        s_ref[4, :, cols] = s
        mx[:, cols] = jnp.maximum(mx[:, cols], fold_max(s))

    for b in range(NB):
        local_scores(b)

    mc = mx[...].max(0, keepdims=True) * (SCALE * LOG2E)

    def prob_far(sx, first):
        for t in range(4):
            cols = slice(t * QT, (t + 1) * QT)
            total = sm[:, cols]
            lo = BLK if first else 0
            dp_ref[sx, lo:, cols] = dot_nt(vf[sx, lo:], cots(t))
            for sy in range(lo // BLK, 4):
                rows = slice(sy * BLK, (sy + 1) * BLK)
                shift = mc[:, cols]
                if first:
                    shift = jnp.where((sy >= 1) & (sy <= y), shift, -NEG)
                p = jnp.exp2(s_ref[sx, rows, cols] * (SCALE * LOG2E) - shift)
                total = total + fold_sum(p)
                p_ref[sx, rows, cols] = p.astype(bf16)
            sm[:, cols] = total
            ot[:, cols] += dot_nn(vt[sx, :, lo:], p_ref[sx, lo:, cols])

    prob_far(0, True)
    pl.loop(1, x + 1)(lambda sx: prob_far(sx, False))
    for b in range(NB):
        cols = slice(b * BLK, (b + 1) * BLK)
        p = jnp.exp2(s_ref[4, :, cols] * (SCALE * LOG2E) - mc[:, cols])
        sm[:, cols] += fold_sum(p)
        p_ref[4, :, cols] = p.astype(bf16)
        ot[:, cols] += dot_nn(vlt[b], p_ref[4, :, cols])

    inv = 1.0 / sm[...].sum(0, keepdims=True)
    deltas = []
    for b in range(NB):
        cols = slice(b * BLK, (b + 1) * BLK)
        o = (ot[:, cols] * inv[:, cols]).T.astype(bf16)
        ao[b, 0] = o
        g = qg[b, 1].astype(f32)
        column = jnp.broadcast_to(inv[:, cols], (BLK, BLK)).T
        gs[cols, :] = (g * column).astype(bf16)
        qs[cols, :] = (qg[b, 0].astype(f32) * (column * SCALE)).astype(bf16)
        deltas.append((g * o.astype(f32)).T.sum(0, keepdims=True))
    delta = jnp.concatenate(deltas, 1)

    def grad_far(sx, first=False):
        lo = BLK if first else 0
        for t in range(4):
            cols = slice(t * QT, (t + 1) * QT)
            for sy in range(lo // BLK, 4):
                rows = slice(sy * BLK, (sy + 1) * BLK)
                d_ref[sx, rows, cols] = p_ref[sx, rows, cols] * (dp_ref[sx, rows, cols] - delta[:, cols]).astype(bf16)
        dqt[...] += dot_nn(kt[sx, :, lo:], d_ref[sx, lo:])
        fv[lo // BLK:, sx] = dot_nn(p_ref[sx, lo:], gs[...]).reshape(4 - lo // BLK, BLK, BLK).astype(bf16)
        fk[sx, lo // BLK:] = dot_nn(d_ref[sx, lo:], qs[...]).reshape(4 - lo // BLK, BLK, BLK).astype(bf16)

    grad_far(0, True)
    pl.loop(1, x + 1)(grad_far)
    for out, far in (((gk0, gk1, gk2a, gk2b, gk3), fk), ((gv0, gv1, gv2a, gv2b, gv3), fv)):
        out[0][...] = far[0]
        out[1][...] = far[1]
        out[2][...] = far[2, :2]
        out[3][...] = far[2, 2:]
        out[4][...] = far[3]
    for b in range(NB):
        cols = slice(b * BLK, (b + 1) * BLK)
        dp = dot_nt(vl[b], qg[b, 1])
        d_ref[4, :, cols] = p_ref[4, :, cols] * (dp - delta[:, cols]).astype(bf16)
        dqt[:, cols] += dot_nn(klt[b], d_ref[4, :, cols])
        dv = dot_nn(p_ref[4, :, cols], gs[cols, :])
        dk = dot_nn(d_ref[4, :, cols], qs[cols, :])
        for i in range(4):
            idx = local[b, i]
            dk_acc[idx] += dk[i * BLK:(i + 1) * BLK]
            dv_acc[idx] += dv[i * BLK:(i + 1) * BLK]
        ao[b, 1] = (dqt[:, cols] * (inv[:, cols] * SCALE)).T.astype(bf16)
    dl[:, 0] = dk_acc[...].astype(bf16)
    dl[:, 1] = dv_acc[...].astype(bf16)
    dsum[0] = dk_acc[sb]
    dsum[1] = dv_acc[sb]


def attention(local, summary, kv, qg, ks, vs):
    width = kv.shape[-1]
    heads = width // BLK

    def block(*lead):
        return pl.BlockSpec((*lead, BLK, BLK), lambda h: (0,) * (len(lead) + 1) + (h,))

    def shape(kind, *lead):
        return jax.ShapeDtypeStruct((*lead, BLK, width), kind)

    smem = pl.BlockSpec(memory_space=pltpu.SMEM)
    counts = [4, 4, 2, 2, 4]
    far = [block(n) for n in counts]
    made = [shape(bf16, n) for n in counts]
    out = pl.pallas_call(
        attention_kernel,
        grid=(heads,),
        in_specs=[smem, smem, block(NB, 2), block(NB, 2)] + far + far,
        out_specs=[block(NB, 2), block(NB, 2), block(2)] + far + far,
        out_shape=[shape(bf16, NB, 2), shape(bf16, NB, 2), shape(f32, 2)] + made + made,
        scratch_shapes=[
            pltpu.VMEM((4, 512, BLK), bf16), pltpu.VMEM((4, 512, BLK), bf16),
            pltpu.VMEM((4, BLK, 512), bf16), pltpu.VMEM((4, BLK, 512), bf16),
            pltpu.VMEM((NB, 512, BLK), bf16), pltpu.VMEM((NB, 512, BLK), bf16),
            pltpu.VMEM((NB, BLK, 512), bf16), pltpu.VMEM((NB, BLK, 512), bf16),
            pltpu.VMEM((5, 512, SPAN), f32), pltpu.VMEM((4, 512, SPAN), f32), pltpu.VMEM((5, 512, SPAN), bf16), pltpu.VMEM((5, 512, SPAN), bf16),
            pltpu.VMEM((8, SPAN), f32), pltpu.VMEM((8, SPAN), f32),
            pltpu.VMEM((BLK, SPAN), f32), pltpu.VMEM((BLK, SPAN), f32),
            pltpu.VMEM((NB, BLK, BLK), f32), pltpu.VMEM((NB, BLK, BLK), f32),
            pltpu.VMEM((SPAN, BLK), bf16), pltpu.VMEM((SPAN, BLK), bf16),
            pltpu.VMEM((4, 4, BLK, BLK), bf16), pltpu.VMEM((4, 4, BLK, BLK), bf16),
        ],
        compiler_params=pltpu.CompilerParams(vmem_limit_bytes=56 << 20),
        cost_estimate=pl.CostEstimate(
            flops=heads * 12 * SPAN * 2432 * BLK, bytes_accessed=heads * (4 << 20), transcendentals=heads * SPAN * 2432
        ),
    )(local, summary, kv, qg, *ks, *vs)
    return out[:3], out[3:8], out[8:]


def through(pairs, held, arrive, leave):
    into = [pltpu.make_async_copy(a, held.at[n], arrive.at[n]) for n, (a, _) in enumerate(pairs)]
    out = [pltpu.make_async_copy(held.at[n], b, leave.at[n]) for n, (_, b) in enumerate(pairs)]
    for copy in into:
        copy.start()
    for before, after in zip(into, out):
        before.wait()
        after.start()
    for copy in out:
        copy.wait()


def pack_kernel(*refs):
    *arrays, out, held, arrive, leave = refs
    width = out.shape[-1]
    through(
        [
            (a.at[:, pl.ds(g * width, width)], out.at[g, i] if len(arrays) > 1 else out.at[g])
            for g in range(NB) for i, a in enumerate(arrays)
        ],
        held, arrive, leave,
    )


def held_blocks(count, width, kind):
    return [pltpu.VMEM((count, BLK, width), kind), pltpu.SemaphoreType.DMA((count,)), pltpu.SemaphoreType.DMA((count,))]


def pack(*arrays):
    width = arrays[0].shape[1] // NB
    lead = (NB, len(arrays)) if len(arrays) > 1 else (NB,)
    return pl.pallas_call(
        pack_kernel,
        in_specs=[pl.BlockSpec(memory_space=pl.ANY)] * len(arrays),
        out_specs=pl.BlockSpec(memory_space=pl.ANY),
        out_shape=jax.ShapeDtypeStruct((*lead, BLK, width), arrays[0].dtype),
        scratch_shapes=held_blocks(NB * len(arrays), width, arrays[0].dtype),
        cost_estimate=pl.CostEstimate(flops=0, bytes_accessed=len(arrays) << 21, transcendentals=0),
    )(*arrays)


def unpack_kernel(got, *refs):
    *arrays, held, arrive, leave = refs
    width = got.shape[-1]
    through(
        [
            (got.at[g, i] if len(arrays) > 1 else got.at[g], a.at[:, pl.ds(g * width, width)])
            for g in range(NB) for i, a in enumerate(arrays)
        ],
        held, arrive, leave,
    )


def unpack(got):
    count, width = (got.shape[1] if got.ndim == 4 else 1), got.shape[-1]
    out = pl.pallas_call(
        unpack_kernel,
        in_specs=[pl.BlockSpec(memory_space=pl.ANY)],
        out_specs=[pl.BlockSpec(memory_space=pl.ANY)] * count,
        out_shape=[jax.ShapeDtypeStruct((BLK, NB * width), got.dtype)] * count,
        scratch_shapes=held_blocks(NB * count, width, got.dtype),
        cost_estimate=pl.CostEstimate(flops=0, bytes_accessed=count << 21, transcendentals=0),
    )(got)
    return out if count > 1 else out[0]


SIDE = 4


def along_x(array, step):
    return lax.ppermute(
        array, "ctx", [(x * SIDE + y, (x + step) % SIDE * SIDE + y) for x in range(SIDE) for y in range(SIDE)]
    )


def along_y(array, step):
    return lax.ppermute(
        array, "ctx", [(x * SIDE + y, x * SIDE + (y + step) % SIDE) for x in range(SIDE) for y in range(SIDE)]
    )


def gather(own, first, second):
    line = jnp.stack([own] + [first(own, s) for s in (1, 2, 3)])
    near = second(line, 1)
    last = second(line, -1)
    return line, near, second(near[:2], 1), second(last[2:], -1), last


def plus(*terms):
    total = terms[0].astype(f32)
    for term in terms[1:]:
        total = total + term.astype(f32)
    return total


def scatter(parts, first, second):
    own, near, low, high, last = parts
    low = second(low, -1)
    high = second(high, 1)
    near = jnp.concatenate([plus(near[:2], low).astype(bf16), near[2:]])
    last = jnp.concatenate([last[:2], plus(last[2:], high).astype(bf16)])
    line = plus(own, second(near, -1), second(last, 1)).astype(bf16)
    return plus(line[0], *[first(line[s], -s) for s in (1, 2, 3)])


def exchange(array):
    return lax.all_to_all(array, "head", split_axis=0, concat_axis=0, tiled=True)


def device_step(queries, keys, values, grad_out, local_blocks, summary_blocks):
    sb = summary_blocks[0, 0]
    kv = exchange(pack(keys, values))
    qg = exchange(pack(queries, grad_out))
    own = lax.dynamic_index_in_dim(kv, sb, 0, keepdims=False)
    ks = gather(own[0], along_y, along_x)
    vs = gather(own[1], along_x, along_y)
    (ao, dl, dsum), fk, fv = attention(local_blocks, summary_blocks, kv, qg, ks, vs)
    attended, grad_q = unpack(exchange(ao))
    far = jnp.stack([scatter(fk, along_y, along_x), scatter(fv, along_x, along_y)])
    dl = lax.dynamic_update_slice(dl, (dsum + far).astype(bf16)[None], (sb, 0, 0, 0))
    grad_k, grad_v = unpack(exchange(dl))
    return attended, grad_q, grad_k, grad_v


def solution(mesh):
    tokens = P(("ctx", "head"), None)
    return jax.shard_map(
        device_step,
        mesh=mesh,
        in_specs=(tokens,) * 4 + (P("ctx", None),) * 2,
        out_specs=(tokens,) * 4,
        check_vma=False,
    )
```

```python
import jax
import jax.numpy as jnp
from jax import lax
from jax.experimental import pallas as pl
from jax.experimental.pallas import tpu as pltpu
from jax.sharding import PartitionSpec as P

BLK = 128
NB = 8
SPAN = 1024
SCALE = 128 ** -0.5
LOG2E = 1.4426950408889634
NEG = -1e30
QT = 256
bf16 = jnp.bfloat16
f32 = jnp.float32


def dot_nt(a, b):
    return lax.dot_general(a, b, (((1,), (1,)), ((), ())), preferred_element_type=f32)


def dot_nn(a, b):
    return lax.dot_general(a, b, (((1,), (0,)), ((), ())), preferred_element_type=f32)


def fold_max(s):
    return s.reshape(s.shape[0] // 8, 8, s.shape[1]).max(0)


def fold_sum(s):
    return s.reshape(s.shape[0] // 8, 8, s.shape[1]).sum(0)


def attention_kernel(
    local, summary, kv, qg, k0, k1, k2a, k2b, k3, v0, v1, v2a, v2b, v3,
    ao, dl, dsum, gk0, gk1, gk2a, gk2b, gk3, gv0, gv1, gv2a, gv2b, gv3,
    kf, vf, kt, vt, kl, vl, klt, vlt, s_ref, dp_ref, p_ref, d_ref, mx, sm, ot, dqt, dk_acc, dv_acc, gs, qs, fk, fv,
):
    span = lax.axis_index("ctx")
    x, y, sb = lax.div(span, 4), lax.rem(span, 4), summary[0, 0]
    for a in range(4):
        for c in range(4):
            rows = slice(c * BLK, (c + 1) * BLK)
            kf[a, rows, :] = ((k0, k1, k2a, k3)[a][c] if a != 2 or c < 2 else k2b[c - 2])
            rows = slice(a * BLK, (a + 1) * BLK)
            vf[c, rows, :] = ((v0, v1, v2a, v3)[a][c] if a != 2 or c < 2 else v2b[c - 2])
    fk[...] = jnp.zeros_like(fk)
    fv[...] = jnp.zeros_like(fv)
    mx[...] = jnp.full_like(mx, NEG)
    sm[...] = jnp.zeros_like(sm)
    ot[...] = jnp.zeros_like(ot)
    dqt[...] = jnp.zeros_like(dqt)
    dk_acc[...] = jnp.zeros_like(dk_acc)
    dv_acc[...] = jnp.zeros_like(dv_acc)

    def queries(t, n=2):
        return qg[t * n:(t + 1) * n, 0].reshape(n * BLK, BLK)

    def cots(t, n=2):
        return qg[t * n:(t + 1) * n, 1].reshape(n * BLK, BLK)

    def score_far(sx, first):
        kt[sx] = kf[sx].T
        vt[sx] = vf[sx].T
        for t in range(4):
            cols = slice(t * QT, (t + 1) * QT)
            lo = BLK if first else 0
            s = dot_nt(kf[sx, lo:], queries(t))
            s_ref[sx, lo:, cols] = s
            if first:
                top = jnp.full((8, QT), NEG, f32)
                for sy in range(1, 4):
                    top = jnp.maximum(top, jnp.where(sy <= y, fold_max(s[sy * BLK - lo:(sy + 1) * BLK - lo]), NEG))
            else:
                top = fold_max(s)
            mx[:, cols] = jnp.maximum(mx[:, cols], top)

    score_far(0, True)
    pl.loop(1, x + 1)(lambda sx: score_far(sx, False))

    def local_scores(b):
        for i in range(4):
            idx = local[b, i]
            kl[b, i * BLK:(i + 1) * BLK, :] = kv[idx, 0]
            vl[b, i * BLK:(i + 1) * BLK, :] = kv[idx, 1]
        klt[b] = kl[b].T
        vlt[b] = vl[b].T
        cols = slice(b * BLK, (b + 1) * BLK)
        s = dot_nt(kl[b], qg[b, 0])
        s_ref[4, :, cols] = s
        mx[:, cols] = jnp.maximum(mx[:, cols], fold_max(s))

    for b in range(NB):
        local_scores(b)

    mc = mx[...].max(0, keepdims=True) * (SCALE * LOG2E)

    def prob_far(sx, first):
        for t in range(4):
            cols = slice(t * QT, (t + 1) * QT)
            total = sm[:, cols]
            lo = BLK if first else 0
            dp_ref[sx, lo:, cols] = dot_nt(vf[sx, lo:], cots(t))
            for sy in range(lo // BLK, 4):
                rows = slice(sy * BLK, (sy + 1) * BLK)
                shift = mc[:, cols]
                if first:
                    shift = jnp.where((sy >= 1) & (sy <= y), shift, -NEG)
                p = jnp.exp2(s_ref[sx, rows, cols] * (SCALE * LOG2E) - shift)
                total = total + fold_sum(p)
                p_ref[sx, rows, cols] = p.astype(bf16)
            sm[:, cols] = total
            ot[:, cols] += dot_nn(vt[sx, :, lo:], p_ref[sx, lo:, cols])

    prob_far(0, True)
    pl.loop(1, x + 1)(lambda sx: prob_far(sx, False))
    for b in range(NB):
        cols = slice(b * BLK, (b + 1) * BLK)
        dp_ref[4, :, cols] = dot_nt(vl[b], qg[b, 1])
        p = jnp.exp2(s_ref[4, :, cols] * (SCALE * LOG2E) - mc[:, cols])
        sm[:, cols] += fold_sum(p)
        p_ref[4, :, cols] = p.astype(bf16)
        ot[:, cols] += dot_nn(vlt[b], p_ref[4, :, cols])

    inv = 1.0 / sm[...].sum(0, keepdims=True)
    deltas = []
    for b in range(NB):
        cols = slice(b * BLK, (b + 1) * BLK)
        o = (ot[:, cols] * inv[:, cols]).T.astype(bf16)
        ao[b, 0] = o
        g = qg[b, 1].astype(f32)
        column = jnp.broadcast_to(inv[:, cols], (BLK, BLK)).T
        gs[cols, :] = (g * column).astype(bf16)
        qs[cols, :] = (qg[b, 0].astype(f32) * (column * SCALE)).astype(bf16)
        deltas.append((g * o.astype(f32)).T.sum(0, keepdims=True))
    delta = jnp.concatenate(deltas, 1)

    def grad_far(sx, first=False):
        lo = BLK if first else 0
        fv[lo // BLK:, sx] = dot_nn(p_ref[sx, lo:], gs[...]).reshape(4 - lo // BLK, BLK, BLK).astype(bf16)
        for t in range(4):
            cols = slice(t * QT, (t + 1) * QT)
            for sy in range(lo // BLK, 4):
                rows = slice(sy * BLK, (sy + 1) * BLK)
                d_ref[sx, rows, cols] = p_ref[sx, rows, cols] * (dp_ref[sx, rows, cols] - delta[:, cols]).astype(bf16)
        dqt[...] += dot_nn(kt[sx, :, lo:], d_ref[sx, lo:])
        fk[sx, lo // BLK:] = dot_nn(d_ref[sx, lo:], qs[...]).reshape(4 - lo // BLK, BLK, BLK).astype(bf16)

    grad_far(0, True)
    pl.loop(1, x + 1)(grad_far)
    for out, far in (((gk0, gk1, gk2a, gk2b, gk3), fk), ((gv0, gv1, gv2a, gv2b, gv3), fv)):
        out[0][...] = far[0]
        out[1][...] = far[1]
        out[2][...] = far[2, :2]
        out[3][...] = far[2, 2:]
        out[4][...] = far[3]
    for b in range(NB):
        cols = slice(b * BLK, (b + 1) * BLK)
        dv = dot_nn(p_ref[4, :, cols], gs[cols, :])
        dp = dp_ref[4, :, cols]
        d_ref[4, :, cols] = p_ref[4, :, cols] * (dp - delta[:, cols]).astype(bf16)
        dqt[:, cols] += dot_nn(klt[b], d_ref[4, :, cols])
        dk = dot_nn(d_ref[4, :, cols], qs[cols, :])
        for i in range(4):
            idx = local[b, i]
            dk_acc[idx] += dk[i * BLK:(i + 1) * BLK]
            dv_acc[idx] += dv[i * BLK:(i + 1) * BLK]
        ao[b, 1] = (dqt[:, cols] * (inv[:, cols] * SCALE)).T.astype(bf16)
    dl[:, 0] = dk_acc[...].astype(bf16)
    dl[:, 1] = dv_acc[...].astype(bf16)
    dsum[0] = dk_acc[sb]
    dsum[1] = dv_acc[sb]


def attention(local, summary, kv, qg, ks, vs):
    width = kv.shape[-1]
    heads = width // BLK

    def block(*lead):
        return pl.BlockSpec((*lead, BLK, BLK), lambda h: (0,) * (len(lead) + 1) + (h,))

    def shape(kind, *lead):
        return jax.ShapeDtypeStruct((*lead, BLK, width), kind)

    smem = pl.BlockSpec(memory_space=pltpu.SMEM)
    counts = [4, 4, 2, 2, 4]
    far = [block(n) for n in counts]
    made = [shape(bf16, n) for n in counts]
    out = pl.pallas_call(
        attention_kernel,
        grid=(heads,),
        in_specs=[smem, smem, block(NB, 2), block(NB, 2)] + far + far,
        out_specs=[block(NB, 2), block(NB, 2), block(2)] + far + far,
        out_shape=[shape(bf16, NB, 2), shape(bf16, NB, 2), shape(f32, 2)] + made + made,
        scratch_shapes=[
            pltpu.VMEM((4, 512, BLK), bf16), pltpu.VMEM((4, 512, BLK), bf16),
            pltpu.VMEM((4, BLK, 512), bf16), pltpu.VMEM((4, BLK, 512), bf16),
            pltpu.VMEM((NB, 512, BLK), bf16), pltpu.VMEM((NB, 512, BLK), bf16),
            pltpu.VMEM((NB, BLK, 512), bf16), pltpu.VMEM((NB, BLK, 512), bf16),
            pltpu.VMEM((5, 512, SPAN), f32), pltpu.VMEM((5, 512, SPAN), f32), pltpu.VMEM((5, 512, SPAN), bf16), pltpu.VMEM((5, 512, SPAN), bf16),
            pltpu.VMEM((8, SPAN), f32), pltpu.VMEM((8, SPAN), f32),
            pltpu.VMEM((BLK, SPAN), f32), pltpu.VMEM((BLK, SPAN), f32),
            pltpu.VMEM((NB, BLK, BLK), f32), pltpu.VMEM((NB, BLK, BLK), f32),
            pltpu.VMEM((SPAN, BLK), bf16), pltpu.VMEM((SPAN, BLK), bf16),
            pltpu.VMEM((4, 4, BLK, BLK), bf16), pltpu.VMEM((4, 4, BLK, BLK), bf16),
        ],
        compiler_params=pltpu.CompilerParams(vmem_limit_bytes=56 << 20),
        cost_estimate=pl.CostEstimate(
            flops=heads * 12 * SPAN * 2432 * BLK, bytes_accessed=heads * (4 << 20), transcendentals=heads * SPAN * 2432
        ),
    )(local, summary, kv, qg, *ks, *vs)
    return out[:3], out[3:8], out[8:]


def through(pairs, held, arrive, leave):
    into = [pltpu.make_async_copy(a, held.at[n], arrive.at[n]) for n, (a, _) in enumerate(pairs)]
    out = [pltpu.make_async_copy(held.at[n], b, leave.at[n]) for n, (_, b) in enumerate(pairs)]
    for copy in into:
        copy.start()
    for before, after in zip(into, out):
        before.wait()
        after.start()
    for copy in out:
        copy.wait()


def pack_kernel(*refs):
    *arrays, out, held, arrive, leave = refs
    width = out.shape[-1]
    through(
        [
            (a.at[:, pl.ds(g * width, width)], out.at[g, i] if len(arrays) > 1 else out.at[g])
            for g in range(NB) for i, a in enumerate(arrays)
        ],
        held, arrive, leave,
    )


def held_blocks(count, width, kind):
    return [pltpu.VMEM((count, BLK, width), kind), pltpu.SemaphoreType.DMA((count,)), pltpu.SemaphoreType.DMA((count,))]


def pack(*arrays):
    width = arrays[0].shape[1] // NB
    lead = (NB, len(arrays)) if len(arrays) > 1 else (NB,)
    return pl.pallas_call(
        pack_kernel,
        in_specs=[pl.BlockSpec(memory_space=pl.ANY)] * len(arrays),
        out_specs=pl.BlockSpec(memory_space=pl.ANY),
        out_shape=jax.ShapeDtypeStruct((*lead, BLK, width), arrays[0].dtype),
        scratch_shapes=held_blocks(NB * len(arrays), width, arrays[0].dtype),
        cost_estimate=pl.CostEstimate(flops=0, bytes_accessed=len(arrays) << 21, transcendentals=0),
    )(*arrays)


def unpack_kernel(got, *refs):
    *arrays, held, arrive, leave = refs
    width = got.shape[-1]
    through(
        [
            (got.at[g, i] if len(arrays) > 1 else got.at[g], a.at[:, pl.ds(g * width, width)])
            for g in range(NB) for i, a in enumerate(arrays)
        ],
        held, arrive, leave,
    )


def unpack(got):
    count, width = (got.shape[1] if got.ndim == 4 else 1), got.shape[-1]
    out = pl.pallas_call(
        unpack_kernel,
        in_specs=[pl.BlockSpec(memory_space=pl.ANY)],
        out_specs=[pl.BlockSpec(memory_space=pl.ANY)] * count,
        out_shape=[jax.ShapeDtypeStruct((BLK, NB * width), got.dtype)] * count,
        scratch_shapes=held_blocks(NB * count, width, got.dtype),
        cost_estimate=pl.CostEstimate(flops=0, bytes_accessed=count << 21, transcendentals=0),
    )(got)
    return out if count > 1 else out[0]


SIDE = 4


def along_x(array, step):
    return lax.ppermute(
        array, "ctx", [(x * SIDE + y, (x + step) % SIDE * SIDE + y) for x in range(SIDE) for y in range(SIDE)]
    )


def along_y(array, step):
    return lax.ppermute(
        array, "ctx", [(x * SIDE + y, x * SIDE + (y + step) % SIDE) for x in range(SIDE) for y in range(SIDE)]
    )


def gather(own, first, second):
    line = jnp.stack([own] + [first(own, s) for s in (1, 2, 3)])
    near = second(line, 1)
    last = second(line, -1)
    return line, near, second(near[:2], 1), second(last[2:], -1), last


def plus(*terms):
    total = terms[0].astype(f32)
    for term in terms[1:]:
        total = total + term.astype(f32)
    return total


def scatter(parts, first, second):
    own, near, low, high, last = parts
    low = second(low, -1)
    high = second(high, 1)
    near = jnp.concatenate([plus(near[:2], low).astype(bf16), near[2:]])
    last = jnp.concatenate([last[:2], plus(last[2:], high).astype(bf16)])
    line = plus(own, second(near, -1), second(last, 1)).astype(bf16)
    return plus(line[0], *[first(line[s], -s) for s in (1, 2, 3)])


def exchange(array):
    return lax.all_to_all(array, "head", split_axis=0, concat_axis=0, tiled=True)


def device_step(queries, keys, values, grad_out, local_blocks, summary_blocks):
    sb = summary_blocks[0, 0]
    kv = exchange(pack(keys, values))
    qg = exchange(pack(queries, grad_out))
    own = lax.dynamic_index_in_dim(kv, sb, 0, keepdims=False)
    ks = gather(own[0], along_y, along_x)
    vs = gather(own[1], along_x, along_y)
    (ao, dl, dsum), fk, fv = attention(local_blocks, summary_blocks, kv, qg, ks, vs)
    attended, grad_q = unpack(exchange(ao))
    far = jnp.stack([scatter(fk, along_y, along_x), scatter(fv, along_x, along_y)])
    dl = lax.dynamic_update_slice(dl, (dsum + far).astype(bf16)[None], (sb, 0, 0, 0))
    grad_k, grad_v = unpack(exchange(dl))
    return attended, grad_q, grad_k, grad_v


def solution(mesh):
    tokens = P(("ctx", "head"), None)
    return jax.shard_map(
        device_step,
        mesh=mesh,
        in_specs=(tokens,) * 4 + (P("ctx", None),) * 2,
        out_specs=(tokens,) * 4,
        check_vma=False,
    )
```

```python
import jax
import jax.numpy as jnp
from jax import lax
from jax.experimental import pallas as pl
from jax.experimental.pallas import tpu as pltpu
from jax.sharding import PartitionSpec as P

BLK = 128
NB = 8
SPAN = 1024
SCALE = 128 ** -0.5
LOG2E = 1.4426950408889634
NEG = -1e30
QT = 256
bf16 = jnp.bfloat16
f32 = jnp.float32


def dot_nt(a, b):
    return lax.dot_general(a, b, (((1,), (1,)), ((), ())), preferred_element_type=f32)


def dot_nn(a, b):
    return lax.dot_general(a, b, (((1,), (0,)), ((), ())), preferred_element_type=f32)


def fold_max(s):
    return s.reshape(s.shape[0] // 8, 8, s.shape[1]).max(0)


def fold_sum(s):
    return s.reshape(s.shape[0] // 8, 8, s.shape[1]).sum(0)


def attention_kernel(
    local, summary, kv, qg, k0, k1, k2a, k2b, k3, v0, v1, v2a, v2b, v3,
    ao, dl, dsum, gk0, gk1, gk2a, gk2b, gk3, gv0, gv1, gv2a, gv2b, gv3,
    kf, vf, kt, vt, kl, vl, klt, vlt, s_ref, dp_ref, p_ref, d_ref, mx, sm, ot, dqt, dk_acc, dv_acc, gs, qs, fk, fv,
):
    span = lax.axis_index("ctx")
    x, y, sb = lax.div(span, 4), lax.rem(span, 4), summary[0, 0]
    for a in range(4):
        for c in range(4):
            rows = slice(c * BLK, (c + 1) * BLK)
            kf[a, rows, :] = ((k0, k1, k2a, k3)[a][c] if a != 2 or c < 2 else k2b[c - 2])
            rows = slice(a * BLK, (a + 1) * BLK)
            vf[c, rows, :] = ((v0, v1, v2a, v3)[a][c] if a != 2 or c < 2 else v2b[c - 2])
    fk[...] = jnp.zeros_like(fk)
    fv[...] = jnp.zeros_like(fv)
    mx[...] = jnp.full_like(mx, NEG)
    sm[...] = jnp.zeros_like(sm)
    ot[...] = jnp.zeros_like(ot)
    dqt[...] = jnp.zeros_like(dqt)
    dk_acc[...] = jnp.zeros_like(dk_acc)
    dv_acc[...] = jnp.zeros_like(dv_acc)

    def queries(t, n=2):
        return qg[t * n:(t + 1) * n, 0].reshape(n * BLK, BLK)

    def cots(t, n=2):
        return qg[t * n:(t + 1) * n, 1].reshape(n * BLK, BLK)

    def score_far(sx, first):
        kt[sx] = kf[sx].T
        vt[sx] = vf[sx].T
        for t in range(4):
            cols = slice(t * QT, (t + 1) * QT)
            lo = BLK if first else 0
            s = dot_nt(kf[sx, lo:], queries(t))
            s_ref[sx, lo:, cols] = s
            if first:
                top = jnp.full((8, QT), NEG, f32)
                for sy in range(1, 4):
                    top = jnp.maximum(top, jnp.where(sy <= y, fold_max(s[sy * BLK - lo:(sy + 1) * BLK - lo]), NEG))
            else:
                top = fold_max(s)
            mx[:, cols] = jnp.maximum(mx[:, cols], top)


    def local_scores(b):
        for i in range(4):
            idx = local[b, i]
            kl[b, i * BLK:(i + 1) * BLK, :] = kv[idx, 0]
            vl[b, i * BLK:(i + 1) * BLK, :] = kv[idx, 1]
        klt[b] = kl[b].T
        vlt[b] = vl[b].T
        cols = slice(b * BLK, (b + 1) * BLK)
        s = dot_nt(kl[b], qg[b, 0])
        s_ref[4, :, cols] = s
        mx[:, cols] = jnp.maximum(mx[:, cols], fold_max(s))

    score_far(0, True)
    for b in range(NB):
        local_scores(b)
    pl.loop(1, x + 1)(lambda sx: score_far(sx, False))

    mc = mx[...].max(0, keepdims=True) * (SCALE * LOG2E)

    def prob_far(sx, first):
        for t in range(4):
            cols = slice(t * QT, (t + 1) * QT)
            total = sm[:, cols]
            lo = BLK if first else 0
            dp_ref[sx, lo:, cols] = dot_nt(vf[sx, lo:], cots(t))
            for sy in range(lo // BLK, 4):
                rows = slice(sy * BLK, (sy + 1) * BLK)
                shift = mc[:, cols]
                if first:
                    shift = jnp.where((sy >= 1) & (sy <= y), shift, -NEG)
                p = jnp.exp2(s_ref[sx, rows, cols] * (SCALE * LOG2E) - shift)
                total = total + fold_sum(p)
                p_ref[sx, rows, cols] = p.astype(bf16)
            sm[:, cols] = total
            ot[:, cols] += dot_nn(vt[sx, :, lo:], p_ref[sx, lo:, cols])

    prob_far(0, True)
    for b in range(NB):
        cols = slice(b * BLK, (b + 1) * BLK)
        dp_ref[4, :, cols] = dot_nt(vl[b], qg[b, 1])
        p = jnp.exp2(s_ref[4, :, cols] * (SCALE * LOG2E) - mc[:, cols])
        sm[:, cols] += fold_sum(p)
        p_ref[4, :, cols] = p.astype(bf16)
        ot[:, cols] += dot_nn(vlt[b], p_ref[4, :, cols])
    pl.loop(1, x + 1)(lambda sx: prob_far(sx, False))

    inv = 1.0 / sm[...].sum(0, keepdims=True)
    deltas = []
    for b in range(NB):
        cols = slice(b * BLK, (b + 1) * BLK)
        o = (ot[:, cols] * inv[:, cols]).T.astype(bf16)
        ao[b, 0] = o
        g = qg[b, 1].astype(f32)
        column = jnp.broadcast_to(inv[:, cols], (BLK, BLK)).T
        gs[cols, :] = (g * column).astype(bf16)
        qs[cols, :] = (qg[b, 0].astype(f32) * (column * SCALE)).astype(bf16)
        deltas.append((g * o.astype(f32)).T.sum(0, keepdims=True))
    delta = jnp.concatenate(deltas, 1)

    def grad_far(sx, first=False):
        lo = BLK if first else 0
        fv[lo // BLK:, sx] = dot_nn(p_ref[sx, lo:], gs[...]).reshape(4 - lo // BLK, BLK, BLK).astype(bf16)
        for t in range(4):
            cols = slice(t * QT, (t + 1) * QT)
            for sy in range(lo // BLK, 4):
                rows = slice(sy * BLK, (sy + 1) * BLK)
                d_ref[sx, rows, cols] = p_ref[sx, rows, cols] * (dp_ref[sx, rows, cols] - delta[:, cols]).astype(bf16)
        dqt[...] += dot_nn(kt[sx, :, lo:], d_ref[sx, lo:])
        fk[sx, lo // BLK:] = dot_nn(d_ref[sx, lo:], qs[...]).reshape(4 - lo // BLK, BLK, BLK).astype(bf16)

    grad_far(0, True)
    for b in range(NB):
        cols = slice(b * BLK, (b + 1) * BLK)
        dv = dot_nn(p_ref[4, :, cols], gs[cols, :])
        dp = dp_ref[4, :, cols]
        d_ref[4, :, cols] = p_ref[4, :, cols] * (dp - delta[:, cols]).astype(bf16)
        dqt[:, cols] += dot_nn(klt[b], d_ref[4, :, cols])
        dk = dot_nn(d_ref[4, :, cols], qs[cols, :])
        for i in range(4):
            idx = local[b, i]
            dk_acc[idx] += dk[i * BLK:(i + 1) * BLK]
            dv_acc[idx] += dv[i * BLK:(i + 1) * BLK]
    pl.loop(1, x + 1)(grad_far)
    for out, far in (((gk0, gk1, gk2a, gk2b, gk3), fk), ((gv0, gv1, gv2a, gv2b, gv3), fv)):
        out[0][...] = far[0]
        out[1][...] = far[1]
        out[2][...] = far[2, :2]
        out[3][...] = far[2, 2:]
        out[4][...] = far[3]
    for b in range(NB):
        cols = slice(b * BLK, (b + 1) * BLK)
        ao[b, 1] = (dqt[:, cols] * (inv[:, cols] * SCALE)).T.astype(bf16)
    dl[:, 0] = dk_acc[...].astype(bf16)
    dl[:, 1] = dv_acc[...].astype(bf16)
    dsum[0] = dk_acc[sb]
    dsum[1] = dv_acc[sb]


def attention(local, summary, kv, qg, ks, vs):
    width = kv.shape[-1]
    heads = width // BLK

    def block(*lead):
        return pl.BlockSpec((*lead, BLK, BLK), lambda h: (0,) * (len(lead) + 1) + (h,))

    def shape(kind, *lead):
        return jax.ShapeDtypeStruct((*lead, BLK, width), kind)

    smem = pl.BlockSpec(memory_space=pltpu.SMEM)
    counts = [4, 4, 2, 2, 4]
    far = [block(n) for n in counts]
    made = [shape(bf16, n) for n in counts]
    out = pl.pallas_call(
        attention_kernel,
        grid=(heads,),
        in_specs=[smem, smem, block(NB, 2), block(NB, 2)] + far + far,
        out_specs=[block(NB, 2), block(NB, 2), block(2)] + far + far,
        out_shape=[shape(bf16, NB, 2), shape(bf16, NB, 2), shape(f32, 2)] + made + made,
        scratch_shapes=[
            pltpu.VMEM((4, 512, BLK), bf16), pltpu.VMEM((4, 512, BLK), bf16),
            pltpu.VMEM((4, BLK, 512), bf16), pltpu.VMEM((4, BLK, 512), bf16),
            pltpu.VMEM((NB, 512, BLK), bf16), pltpu.VMEM((NB, 512, BLK), bf16),
            pltpu.VMEM((NB, BLK, 512), bf16), pltpu.VMEM((NB, BLK, 512), bf16),
            pltpu.VMEM((5, 512, SPAN), f32), pltpu.VMEM((5, 512, SPAN), f32), pltpu.VMEM((5, 512, SPAN), bf16), pltpu.VMEM((5, 512, SPAN), bf16),
            pltpu.VMEM((8, SPAN), f32), pltpu.VMEM((8, SPAN), f32),
            pltpu.VMEM((BLK, SPAN), f32), pltpu.VMEM((BLK, SPAN), f32),
            pltpu.VMEM((NB, BLK, BLK), f32), pltpu.VMEM((NB, BLK, BLK), f32),
            pltpu.VMEM((SPAN, BLK), bf16), pltpu.VMEM((SPAN, BLK), bf16),
            pltpu.VMEM((4, 4, BLK, BLK), bf16), pltpu.VMEM((4, 4, BLK, BLK), bf16),
        ],
        compiler_params=pltpu.CompilerParams(vmem_limit_bytes=56 << 20),
        cost_estimate=pl.CostEstimate(
            flops=heads * 12 * SPAN * 2432 * BLK, bytes_accessed=heads * (4 << 20), transcendentals=heads * SPAN * 2432
        ),
    )(local, summary, kv, qg, *ks, *vs)
    return out[:3], out[3:8], out[8:]


def through(pairs, held, arrive, leave):
    into = [pltpu.make_async_copy(a, held.at[n], arrive.at[n]) for n, (a, _) in enumerate(pairs)]
    out = [pltpu.make_async_copy(held.at[n], b, leave.at[n]) for n, (_, b) in enumerate(pairs)]
    for copy in into:
        copy.start()
    for before, after in zip(into, out):
        before.wait()
        after.start()
    for copy in out:
        copy.wait()


def pack_kernel(*refs):
    *arrays, out, held, arrive, leave = refs
    width = out.shape[-1]
    through(
        [
            (a.at[:, pl.ds(g * width, width)], out.at[g, i] if len(arrays) > 1 else out.at[g])
            for g in range(NB) for i, a in enumerate(arrays)
        ],
        held, arrive, leave,
    )


def held_blocks(count, width, kind):
    return [pltpu.VMEM((count, BLK, width), kind), pltpu.SemaphoreType.DMA((count,)), pltpu.SemaphoreType.DMA((count,))]


def pack(*arrays):
    width = arrays[0].shape[1] // NB
    lead = (NB, len(arrays)) if len(arrays) > 1 else (NB,)
    return pl.pallas_call(
        pack_kernel,
        in_specs=[pl.BlockSpec(memory_space=pl.ANY)] * len(arrays),
        out_specs=pl.BlockSpec(memory_space=pl.ANY),
        out_shape=jax.ShapeDtypeStruct((*lead, BLK, width), arrays[0].dtype),
        scratch_shapes=held_blocks(NB * len(arrays), width, arrays[0].dtype),
        cost_estimate=pl.CostEstimate(flops=0, bytes_accessed=len(arrays) << 21, transcendentals=0),
    )(*arrays)


def unpack_kernel(got, *refs):
    *arrays, held, arrive, leave = refs
    width = got.shape[-1]
    through(
        [
            (got.at[g, i] if len(arrays) > 1 else got.at[g], a.at[:, pl.ds(g * width, width)])
            for g in range(NB) for i, a in enumerate(arrays)
        ],
        held, arrive, leave,
    )


def unpack(got):
    count, width = (got.shape[1] if got.ndim == 4 else 1), got.shape[-1]
    out = pl.pallas_call(
        unpack_kernel,
        in_specs=[pl.BlockSpec(memory_space=pl.ANY)],
        out_specs=[pl.BlockSpec(memory_space=pl.ANY)] * count,
        out_shape=[jax.ShapeDtypeStruct((BLK, NB * width), got.dtype)] * count,
        scratch_shapes=held_blocks(NB * count, width, got.dtype),
        cost_estimate=pl.CostEstimate(flops=0, bytes_accessed=count << 21, transcendentals=0),
    )(got)
    return out if count > 1 else out[0]


SIDE = 4


def along_x(array, step):
    return lax.ppermute(
        array, "ctx", [(x * SIDE + y, (x + step) % SIDE * SIDE + y) for x in range(SIDE) for y in range(SIDE)]
    )


def along_y(array, step):
    return lax.ppermute(
        array, "ctx", [(x * SIDE + y, x * SIDE + (y + step) % SIDE) for x in range(SIDE) for y in range(SIDE)]
    )


def gather(own, first, second):
    line = jnp.stack([own] + [first(own, s) for s in (1, 2, 3)])
    near = second(line, 1)
    last = second(line, -1)
    return line, near, second(near[:2], 1), second(last[2:], -1), last


def plus(*terms):
    total = terms[0].astype(f32)
    for term in terms[1:]:
        total = total + term.astype(f32)
    return total


def scatter(parts, first, second):
    own, near, low, high, last = parts
    low = second(low, -1)
    high = second(high, 1)
    near = jnp.concatenate([plus(near[:2], low).astype(bf16), near[2:]])
    last = jnp.concatenate([last[:2], plus(last[2:], high).astype(bf16)])
    line = plus(own, second(near, -1), second(last, 1)).astype(bf16)
    return plus(line[0], *[first(line[s], -s) for s in (1, 2, 3)])


def exchange(array):
    return lax.all_to_all(array, "head", split_axis=0, concat_axis=0, tiled=True)


def device_step(queries, keys, values, grad_out, local_blocks, summary_blocks):
    sb = summary_blocks[0, 0]
    kv = exchange(pack(keys, values))
    qg = exchange(pack(queries, grad_out))
    own = lax.dynamic_index_in_dim(kv, sb, 0, keepdims=False)
    ks = gather(own[0], along_y, along_x)
    vs = gather(own[1], along_x, along_y)
    (ao, dl, dsum), fk, fv = attention(local_blocks, summary_blocks, kv, qg, ks, vs)
    attended, grad_q = unpack(exchange(ao))
    far = jnp.stack([scatter(fk, along_y, along_x), scatter(fv, along_x, along_y)])
    dl = lax.dynamic_update_slice(dl, (dsum + far).astype(bf16)[None], (sb, 0, 0, 0))
    grad_k, grad_v = unpack(exchange(dl))
    return attended, grad_q, grad_k, grad_v


def solution(mesh):
    tokens = P(("ctx", "head"), None)
    return jax.shard_map(
        device_step,
        mesh=mesh,
        in_specs=(tokens,) * 4 + (P("ctx", None),) * 2,
        out_specs=(tokens,) * 4,
        check_vma=False,
    )
```
